32 devices in a mesh: parts: 2 (over y), blk: 4 (over z), fsdp: 2 (over x), dp: 2 (over core).
Axes of the slice: x: 2, y: 2, z: 4, core: 2. Of those that a mesh axis runs over, the one named last changes fastest.
Arguments:
- tokens: bfloat16 [3072, 2304], P(('parts', 'blk', 'dp'), 'fsdp'), parts along dimension 0, may hold values from -6 to 6
- targets: bfloat16 [3072, 4, 2304], P(('parts', 'blk', 'dp'), None, 'fsdp'), parts along dimension 0, may hold values from -6 to 6
- enc_weight: bfloat16 [2304, 16384], P('fsdp', 'blk'), may hold values from -0.125 to 0.125
- enc_bias: float32 [16384], P('blk'), may hold values from -3 to 3
- dec_weight: bfloat16 [4, 16384, 2304], P(None, 'blk', 'fsdp'), may hold values from -0.046875 to 0.046875
- active_blocks: int32 [24, 32], P('parts'), parts along dimension 0, may hold values from 0 to 127, as said below
Outputs:
- enc_grad: bfloat16 [4608, 16384], P(('parts', 'fsdp', 'dp'), 'blk'), parts along dimension 0
- dec_grad: bfloat16 [8, 16384, 2304], P('parts', 'blk', ('fsdp', 'dp')), parts along dimension 0
The draws below stay inside these ranges and needn't reach their ends.
There are 2 independent parts, one for each index of `parts`. The reference program is written for one: setup_inputs(seed, part) draws one part's arguments, and reference() takes and returns one part's arrays. A program takes and returns all parts, laid end to end along the dimension named above; an argument that names none is the same for every part. Nothing has to cross between parts.
Inputs may be any that keep to these rules, and one draw needn't show every extreme that they name: `active_blocks`: each row lists 32 different latent blocks; every latent block is listed by some row.
All inputs are finite; a program needn't handle non-finite values.
Results may differ from the reference program's by a relative error of at most 0.022.
Values may be sent and summed in bfloat16 or wider, within the bound.
A program may use at most 320 MiB of HBM per device.

```python
import jax
import jax.numpy as jnp
from jax import lax

D = 2304
F = 16384
LATBLK = 128
TOKBLK = 128
ACTIVE = 32
TARGETS = 4
CYCLE_TOK = 768
TOKENS = 1536
TOK_DEV = 192
TBLOCKS = 12
LBLOCKS = 128
PANELS = 2
N_BLK = 4
N_DP = 2


def draw_active_blocks(key, part):
    key = jax.random.fold_in(key, 11)
    key_order, key_level, key_noise = jax.random.split(key, 3)
    order = jax.random.permutation(key_order, LBLOCKS).astype(jnp.int32)
    rows = jnp.arange(TBLOCKS, dtype=jnp.int32)
    slots = jnp.arange(ACTIVE, dtype=jnp.int32)
    position = rows[:, None] * ACTIVE + slots[None, :]
    listed = order[position % LBLOCKS]
    in_cover = position < LBLOCKS
    every_block = jnp.arange(LBLOCKS, dtype=jnp.int32)
    cover = jnp.any((listed[:, :, None] == every_block[None, None, :]) & in_cover[:, :, None], axis=1).astype(jnp.int32)
    popular = jax.random.randint(key_level, (LBLOCKS,), 0, 4, dtype=jnp.int32)
    noise = jax.random.randint(key_noise, (TBLOCKS, LBLOCKS), 0, 65536, dtype=jnp.int32)
    score = (noise + popular[None, :] * 65536 + cover * 262144) * LBLOCKS + every_block[None, :]
    unused, picked = lax.top_k(score, ACTIVE)
    return picked.astype(jnp.int32)


def levels(own_key, extent, cuts, low, largest):
    def one(dim, blocks):
        heights = jax.random.uniform(jax.random.fold_in(jax.random.fold_in(own_key, 6), dim), (blocks,), jnp.float32, low / len(cuts), largest / len(cuts))
        return jnp.repeat(jnp.exp(heights), extent[dim] // blocks).reshape((-1,) + (1,) * (len(extent) - dim - 1))

    factor_of = one(*cuts[0])
    for cut in cuts[1:]:
        factor_of = factor_of * one(*cut)
    return factor_of


def normal_values(key, extent, deviation, most, cuts=(), kind=jnp.bfloat16):
    array = deviation * jax.random.normal(key, extent, jnp.float32)
    if cuts:
        array = array * levels(key, extent, cuts, -0.22, 0.18)
    return jnp.clip(array, -most, most).astype(kind)


def setup_inputs(seed: int = 0, part: int = 0) -> dict:
    seeds = jax.random.split(jax.random.key(seed), 7)
    part_keys = jax.random.split(jax.random.fold_in(seeds[6], part), 7)
    tokens = normal_values(part_keys[0], (TOKENS, D), 1.0, 6.0, ((0, 8), (1, 2)))
    targets = normal_values(part_keys[1], (TOKENS, TARGETS, D), 1.0, 6.0, ((0, 8), (2, 2)))
    enc_weight = normal_values(seeds[2], (D, F), D ** -0.5, 0.125, ((0, 2), (1, 4)))
    enc_bias = normal_values(seeds[3], (F,), 0.5, 3.0, ((0, 4),), jnp.float32)
    dec_weight = normal_values(seeds[4], (TARGETS, F, D), F ** -0.5, 0.046875, ((1, 4), (2, 2)))
    active_blocks = draw_active_blocks(jax.random.fold_in(jax.random.fold_in(seeds[6], part), 71), part)
    return {"tokens": tokens, "targets": targets, "enc_weight": enc_weight, "enc_bias": enc_bias, "dec_weight": dec_weight, "active_blocks": active_blocks}


def settle(values):
    return lax.optimization_barrier(values.astype(jnp.bfloat16)).astype(jnp.float32)


def reference(tokens, targets, enc_weight, enc_bias, dec_weight, active_blocks):
    panel_width = D // PANELS
    row_block = jnp.arange(TOKENS, dtype=jnp.int32) // TOKBLK
    col_block = jnp.arange(F, dtype=jnp.int32) // LATBLK
    present = jnp.any(active_blocks[:, :, None] == col_block[None, None, :], axis=1).astype(jnp.float32)
    onehot = (row_block[:, None] == jnp.arange(TBLOCKS, dtype=jnp.int32)[None, :]).astype(jnp.float32)
    latent_on = jnp.dot(onehot, present, precision=lax.Precision.HIGHEST)
    pre_sum = jnp.zeros((TOKENS, F), jnp.float32)
    for panel_idx in range(PANELS):
        lower = panel_idx * panel_width
        upper = lower + panel_width
        part = jnp.dot(tokens[:, lower:upper], enc_weight[lower:upper], preferred_element_type=jnp.float32)
        pre_sum = pre_sum + settle(part)
    preact = pre_sum + enc_bias
    positive = jnp.maximum(preact, 0.0)
    activations = (latent_on * positive * positive).astype(jnp.bfloat16)
    rebuilt = jnp.stack([jnp.dot(activations, dec_weight[target_idx], preferred_element_type=jnp.float32) for target_idx in range(TARGETS)], axis=1)
    residual_grad = ((2.0 / TBLOCKS) * (rebuilt - targets.astype(jnp.float32))).astype(jnp.bfloat16)
    act_grad = jnp.zeros((TOKENS, F), jnp.float32)
    for panel_idx in range(PANELS):
        lower = panel_idx * panel_width
        upper = lower + panel_width
        part = jnp.zeros((TOKENS, F), jnp.float32)
        for target_idx in range(TARGETS):
            part = part + jnp.dot(residual_grad[:, target_idx, lower:upper], dec_weight[target_idx, :, lower:upper].T, preferred_element_type=jnp.float32)
        act_grad = act_grad + settle(part)
    pre_grad = (act_grad * latent_on * 2.0 * positive).astype(jnp.bfloat16)
    enc_total = jnp.zeros((D, F), jnp.float32)
    dec_total = jnp.zeros((TARGETS, F, D), jnp.float32)
    for pair_idx in range(N_DP):
        tok_pair = tokens.reshape(N_BLK, N_DP, TOK_DEV, D)[:, pair_idx].reshape(CYCLE_TOK, D)
        grad_pair = pre_grad.reshape(N_BLK, N_DP, TOK_DEV, F)[:, pair_idx].reshape(CYCLE_TOK, F)
        act_pair = activations.reshape(N_BLK, N_DP, TOK_DEV, F)[:, pair_idx].reshape(CYCLE_TOK, F)
        res_pair = residual_grad.reshape(N_BLK, N_DP, TOK_DEV, TARGETS, D)[:, pair_idx].reshape(CYCLE_TOK, TARGETS, D)
        enc_total = enc_total + settle(jnp.dot(tok_pair.T, grad_pair, preferred_element_type=jnp.float32))
        dec_term = jnp.stack([jnp.dot(act_pair.T, res_pair[:, target_idx], preferred_element_type=jnp.float32) for target_idx in range(TARGETS)], axis=0)
        dec_total = dec_total + settle(dec_term)
    return (enc_total.astype(jnp.bfloat16), dec_total.astype(jnp.bfloat16))
```

```python
import functools

import jax
import jax.numpy as jnp
import numpy as np
from jax import lax
from jax.experimental import pallas as pl
from jax.experimental.pallas import tpu as pltpu
from jax.sharding import PartitionSpec as P

LATBLK = 128
TOKBLK = 128
F32 = jnp.float32
BF16 = jnp.bfloat16
VMEM_LIMIT = 32 * 1024 * 1024


def swapped(block, axis, bit):
    count = lax.axis_size(axis)
    route = []
    for low in range(count):
        high = low | 1 << bit
        if high != low and high < count:
            route += [(low, high), (high, low)]
    return lax.ppermute(block, axis, route)


def dense_tail(
    group_tokens, targets, enc_weight, enc_bias, dec_weight, active_blocks
):
    tok_rows = targets.shape[0]
    latent_cols = enc_weight.shape[1]
    data_count = lax.axis_size("dp")
    shard_index = lax.axis_index("blk")
    pair_index = lax.axis_index("dp")
    token_blocks = active_blocks.shape[0]
    grad_scale = 2.0 / token_blocks
    group_rows = group_tokens.shape[0]
    positions = jnp.arange(group_rows, dtype=jnp.int32)
    source_dev = positions // tok_rows
    global_row = (source_dev * data_count + pair_index) * tok_rows + positions % tok_rows
    row_block = global_row // TOKBLK
    row_onehot = (row_block[:, None] == jnp.arange(token_blocks, dtype=jnp.int32)[None, :]).astype(F32)
    partial_value = jnp.dot(group_tokens, enc_weight, preferred_element_type=F32)
    pre_total = lax.psum(partial_value.astype(BF16), "fsdp").astype(F32)
    positive = jnp.maximum(pre_total + enc_bias, 0.0)
    col_block = (shard_index * latent_cols + jnp.arange(latent_cols, dtype=jnp.int32)) // LATBLK
    present = jnp.any(active_blocks[:, :, None] == col_block[None, None, :], axis=1).astype(F32)
    latent_on = jnp.dot(row_onehot, present, preferred_element_type=F32)
    activations = (latent_on * positive * positive).astype(BF16)
    rebuilt = lax.psum_scatter(
        jnp.einsum("tf,kfj->tkj", activations, dec_weight, preferred_element_type=F32).astype(BF16),
        "blk",
        scatter_dimension=0,
        tiled=True,
    ).astype(F32)
    own_grad = (grad_scale * (rebuilt - targets.astype(F32))).astype(BF16)
    residual_grad = lax.all_gather(own_grad, "blk", axis=0, tiled=True)
    back_part = jnp.einsum("tkj,kfj->tf", residual_grad, dec_weight, preferred_element_type=F32)
    act_grad = lax.psum(back_part.astype(BF16), "fsdp").astype(F32)
    pre_grad = (act_grad * latent_on * 2.0 * positive).astype(BF16)
    return weight_grads(group_tokens, pre_grad, activations, residual_grad)


def weight_grads(group_tokens, pre_grad, activations, residual_grad):
    pair_index = lax.axis_index("dp")
    half = group_tokens.shape[1] // 2
    keep_start = pair_index * half
    send_start = (1 - pair_index) * half

    def dec_of(start):
        part = lax.dynamic_slice_in_dim(residual_grad, start, half, 2)
        return jnp.einsum("tf,tkj->kfj", activations, part, preferred_element_type=F32).astype(BF16)

    def enc_of(start):
        part = lax.dynamic_slice_in_dim(group_tokens, start, half, 1)
        return jnp.einsum("ti,tf->if", part, pre_grad, preferred_element_type=F32).astype(BF16)

    got_dec = swapped(dec_of(send_start), "dp", 0)
    keep_dec = dec_of(keep_start)
    got_enc = swapped(enc_of(send_start), "dp", 0)
    keep_enc = enc_of(keep_start)
    enc_grad = (keep_enc.astype(F32) + got_enc.astype(F32)).astype(BF16)
    dec_grad = (keep_dec.astype(F32) + got_dec.astype(F32)).astype(BF16)
    return (enc_grad, dec_grad)


def tile_at(code, lat_blocks, unit):
    row = pl.multiple_of((code // lat_blocks) * unit, unit)
    col = pl.multiple_of((code % lat_blocks) * LATBLK, LATBLK)
    return pl.ds(row, unit), pl.ds(col, LATBLK)


def pack_kernel(lat_blocks, unit, code_ref, dense_ref, packed_ref):
    @pl.loop(0, packed_ref.shape[0])
    def _(slot):
        rows, cols = tile_at(code_ref[slot], lat_blocks, unit)
        packed_ref[slot] = dense_ref[rows, cols]


def act_kernel(lat_blocks, unit, code_ref, mine_ref, other_ref, bias_ref, act_ref):
    act_ref[...] = jnp.zeros_like(act_ref)

    @pl.loop(0, code_ref[mine_ref.shape[0]])
    def _(slot):
        rows, cols = tile_at(code_ref[slot], lat_blocks, unit)
        pre = mine_ref[slot].astype(F32) + other_ref[slot].astype(F32) + bias_ref[:, cols]
        positive = jnp.maximum(pre, 0.0)
        act_ref[rows, cols] = (positive * positive).astype(BF16)


def pre_grad_kernel(
    lat_blocks, unit, code_ref, mine_ref, other_ref, bias_ref, back_mine_ref, back_other_ref, out_ref
):
    out_ref[...] = jnp.zeros_like(out_ref)

    @pl.loop(0, code_ref[mine_ref.shape[0]])
    def _(slot):
        rows, cols = tile_at(code_ref[slot], lat_blocks, unit)
        pre = mine_ref[slot].astype(F32) + other_ref[slot].astype(F32) + bias_ref[:, cols]
        grad = back_mine_ref[slot].astype(F32) + back_other_ref[slot].astype(F32)
        out_ref[rows, cols] = (grad * (2.0 * jnp.maximum(pre, 0.0))).astype(BF16)


def on_tiles(kernel, out_shape, codes, *arrays):
    size = out_shape.size * 2 + sum(array.size * array.dtype.itemsize for array in arrays)
    return pl.pallas_call(
        kernel,
        out_shape=out_shape,
        in_specs=[pl.BlockSpec(memory_space=pltpu.SMEM)]
        + [pl.BlockSpec(memory_space=pltpu.VMEM)] * len(arrays),
        out_specs=pl.BlockSpec(memory_space=pltpu.VMEM),
        compiler_params=pltpu.CompilerParams(vmem_limit_bytes=VMEM_LIMIT),
        cost_estimate=pl.CostEstimate(flops=out_shape.size * 4, bytes_accessed=size, transcendentals=0),
    )(codes, *arrays)


def other_panels(packed):
    count = lax.axis_size("fsdp")
    if count == 2:
        return swapped(packed, "fsdp", 0)
    total = lax.psum(packed.astype(F32), "fsdp")
    return total - packed.astype(F32)


def shifted(block, axis, up, senders):
    step = 1 if up else -1
    return lax.ppermute(block, axis, [(dev, dev + step) for dev in senders])


def scatter_sum(parts):
    count = lax.axis_size("blk")
    me = lax.axis_index("blk")

    def term(owner):
        return lax.dynamic_index_in_dim(parts, jnp.clip(owner, 0, count - 1), 0, keepdims=False)

    total = term(me).astype(F32)
    for up in (True, False):
        held = None
        for step in range(1, count):
            owner = me + count - step if up else me - count + step
            block = term(owner)
            if held is not None:
                block = (block.astype(F32) + held.astype(F32)).astype(BF16)
            senders = range(0, step) if up else range(count - step, count)
            held = shifted(block, "blk", up, senders)
        if held is not None:
            total = total + held.astype(F32)
    return total


def gather_line(own):
    count = lax.axis_size("blk")
    me = lax.axis_index("blk")
    below, above = [], []
    for up, got in ((True, below), (False, above)):
        held = own
        for step in range(1, count):
            senders = range(step - 1, count - 1) if up else range(1, count - step + 1)
            held = shifted(held, "blk", up, senders)
            got.append(held)
    line = jnp.stack(below[::-1] + [own] + above)
    return lax.dynamic_slice_in_dim(line, count - 1 - me, count, 0)


def listed_tail(capacity, group_tokens, targets, enc_weight, enc_bias, dec_weight, present):
    tok_rows = targets.shape[0]
    latent_cols = enc_weight.shape[1]
    count = lax.axis_size("blk")
    data_count = lax.axis_size("dp")
    shard_index = lax.axis_index("blk")
    pair_index = lax.axis_index("dp")
    token_blocks = present.shape[0]
    grad_scale = 2.0 / token_blocks
    unit = int(np.gcd(tok_rows, TOKBLK))
    chunks = tok_rows // unit
    lat_blocks = latent_cols // LATBLK
    bias = enc_bias.reshape(1, latent_cols)
    by_dev = group_tokens.reshape(count, tok_rows, -1)
    rows = count * unit
    packed_shape = jax.ShapeDtypeStruct((capacity, unit, LATBLK), BF16)
    dense_shape = jax.ShapeDtypeStruct((rows, latent_cols), BF16)
    own_present = lax.dynamic_slice_in_dim(present, shard_index * lat_blocks, lat_blocks, 1)
    slots = jnp.arange(capacity, dtype=jnp.int32)

    def tiled(kernel):
        return functools.partial(kernel, lat_blocks, unit)

    codes, tokens_of, mine, other = [], [], [], []
    for chunk in range(chunks):
        first_row = (jnp.arange(count, dtype=jnp.int32) * data_count + pair_index) * tok_rows + chunk * unit
        onehot = (first_row // TOKBLK)[:, None] == jnp.arange(token_blocks, dtype=jnp.int32)[None, :]
        on = jnp.any(onehot[:, :, None] & own_present[None], axis=1).reshape(-1)
        index = jnp.arange(on.shape[0], dtype=jnp.int32)
        before = jnp.sum((on[None, :] & (index[None, :] < index[:, None])).astype(jnp.int32), axis=1)
        hit = on[None, :] & (before[None, :] == slots[:, None])
        code = jnp.sum(jnp.where(hit, index[None, :], 0), axis=1)
        codes.append(jnp.concatenate([code, jnp.sum(on.astype(jnp.int32))[None]]))
        tokens_of.append(by_dev[:, chunk * unit : (chunk + 1) * unit].reshape(rows, -1))
    for chunk in range(chunks):
        part = jnp.dot(tokens_of[chunk], enc_weight, preferred_element_type=F32).astype(BF16)
        mine.append(on_tiles(tiled(pack_kernel), packed_shape, codes[chunk], part))
        other.append(other_panels(mine[chunk]))
    acts, sums = [], []
    for chunk in range(chunks):
        acts.append(on_tiles(tiled(act_kernel), dense_shape, codes[chunk], mine[chunk], other[chunk], bias))
        part = jnp.einsum("tf,kfj->tkj", acts[chunk], dec_weight, preferred_element_type=F32).astype(BF16)
        sums.append(scatter_sum(part.reshape(count, unit, *part.shape[1:])))
    residuals, pre_grads = [], []
    for chunk in range(chunks):
        goal = targets[chunk * unit : (chunk + 1) * unit].astype(F32)
        own_grad = (grad_scale * (sums[chunk] - goal)).astype(BF16)
        line = gather_line(own_grad)
        residuals.append(line.reshape(rows, *line.shape[2:]))
    for chunk in range(chunks):
        back = jnp.einsum("tkj,kfj->tf", residuals[chunk], dec_weight, preferred_element_type=F32).astype(BF16)
        back_mine = on_tiles(tiled(pack_kernel), packed_shape, codes[chunk], back)
        back_other = other_panels(back_mine)
        pre_grads.append(
            on_tiles(
                tiled(pre_grad_kernel), dense_shape, codes[chunk], mine[chunk], other[chunk], bias,
                back_mine, back_other,
            )
        )
    return weight_grads(
        jnp.concatenate(tokens_of), jnp.concatenate(pre_grads), jnp.concatenate(acts), jnp.concatenate(residuals)
    )


def most_listed(present, tok_rows):
    count = lax.axis_size("blk")
    data_count = lax.axis_size("dp")
    unit = int(np.gcd(tok_rows, TOKBLK))
    chunks = tok_rows // unit
    per_shard = jnp.sum(present.reshape(present.shape[0], count, -1).astype(F32), axis=2)
    members = np.zeros((data_count * chunks, present.shape[0]), np.float32)
    for dev in range(count):
        for pair in range(data_count):
            for chunk in range(chunks):
                row = (dev * data_count + pair) * tok_rows + chunk * unit
                members[pair * chunks + chunk, row // TOKBLK] += 1.0
    return jnp.max(jnp.sum(members[:, :, None] * per_shard[None], axis=1)).astype(jnp.int32)


def on_device(tokens, targets, enc_weight, enc_bias, dec_weight, active_blocks):
    tok_rows = tokens.shape[0]
    lat_blocks = enc_weight.shape[1] // LATBLK
    all_blocks = lat_blocks * lax.axis_size("blk")
    present = jnp.any(
        active_blocks[:, :, None] == jnp.arange(all_blocks, dtype=jnp.int32)[None, None, :], axis=1
    )
    tiles = lax.axis_size("blk") * lat_blocks
    capacity = tiles * 7 // 16
    most = lax.pmax(most_listed(present, tok_rows), "parts")
    group_tokens = lax.all_gather(tokens, "blk", axis=0, tiled=True)
    return lax.cond(
        most <= capacity,
        lambda: listed_tail(capacity, group_tokens, targets, enc_weight, enc_bias, dec_weight, present),
        lambda: dense_tail(group_tokens, targets, enc_weight, enc_bias, dec_weight, active_blocks),
    )


def solution(mesh):
    return jax.shard_map(
        on_device,
        mesh=mesh,
        in_specs=(
            P(("parts", "blk", "dp"), "fsdp"),
            P(("parts", "blk", "dp"), None, "fsdp"),
            P("fsdp", "blk"),
            P("blk"),
            P(None, "blk", "fsdp"),
            P("parts", None),
        ),
        out_specs=(P(("parts", "fsdp", "dp"), "blk"), P("parts", "blk", ("fsdp", "dp"))),
        check_vma=False,
    )
```
